256 devices in a mesh: dp: 32 (over x, z_hi, core), tensor: 8 (over z_lo, y).
Axes of the slice: x: 4, y: 4, z: 8 (z_hi: 4, z_lo: 2; z = z_hi * 2 + z_lo), core: 2. Of those that a mesh axis runs over, the one named last changes fastest.
Arguments:
- acts: bfloat16 [16384, 4096], P('dp'), may hold values from -6 to 6
- output_grad: bfloat16 [16384, 4096], P('dp'), may hold values from -16 to 16
- gate_act: bfloat16 [16384, 14336], P('dp', 'tensor'), may hold values from -8 to 8
- down_weight: bfloat16 [14336, 4096], P('tensor', 'dp'), may hold values from -0.09375 to 0.09375
- proj_in: bfloat16 [64, 4096], replicated, may hold values from -0.09375 to 0.09375
- proj_out: bfloat16 [64, 14336], P(None, 'tensor'), may hold values from -0.046875 to 0.046875
- query: bfloat16 [1024, 4096], P('tensor', 'dp'), may hold values from -6 to 6
Outputs:
- gram: float32 [4096, 4096], P('dp', 'tensor')
- scores: float32 [64, 1024], P('dp', 'tensor')
The draws below stay inside these ranges and needn't reach their ends.
All inputs are finite; a program needn't handle non-finite values.
Results may differ from the reference program's by a relative error of at most 0.0057.
Values may be sent and summed in bfloat16 or wider, within the bound.
No kernel may reach another device: no remote copies, remote signals or barrier semaphores. Data moves between devices by JAX's collectives and lax.ppermute only.
A program may use at most 128 MiB of HBM per device.

```python
import jax
import jax.numpy as jnp
from jax import lax

D = 4096
FF = 14336
K_IN = 64
K_OUT = 64
NQ = 1024
EX_DEV = 2
SEQ = 256
SK = 4096
TOK_DEV = 512
EXAMPLES = 64
TOKENS = 16384
N_DP = 32


def draw_output_grad(key, part):
    key = jax.random.fold_in(key, 5)
    base_key, spread_key = jax.random.split(key)
    position = jnp.arange(EXAMPLES, dtype=jnp.float32) / (EXAMPLES - 1)
    spread = jax.random.uniform(spread_key, (EXAMPLES,), dtype=jnp.float32)
    base = jnp.clip(jax.random.normal(base_key, (TOKENS, D), dtype=jnp.float32), -5.0, 5.0)
    rising = 3.0 ** position
    scale = jnp.sqrt(rising * 3.3 ** spread)
    row_scale = jnp.repeat(scale, SEQ)
    return (base * row_scale[:, None]).astype(jnp.bfloat16)


def levels(rng, dims, cuts, smallest, top_value):
    def one(dim, blocks):
        heights = jax.random.uniform(jax.random.fold_in(jax.random.fold_in(rng, 6), dim), (blocks,), jnp.float32, smallest / len(cuts), top_value / len(cuts))
        return jnp.repeat(jnp.exp(heights), dims[dim] // blocks).reshape((-1,) + (1,) * (len(dims) - dim - 1))

    level = one(*cuts[0])
    for cut in cuts[1:]:
        level = level * one(*cut)
    return level


def scatter_about(own_key, extent, scale, most, cuts=(), kind=jnp.bfloat16):
    values = scale * jax.random.normal(own_key, extent, jnp.float32)
    if cuts:
        values = values * levels(own_key, extent, cuts, -0.22, 0.18)
    return jnp.clip(values, -most, most).astype(kind)


def setup_inputs(seed: int = 0) -> dict:
    splits = jax.random.split(jax.random.key(seed), 8)
    return {
        "acts": scatter_about(splits[0], (TOKENS, D), 1.0, 6.0, ((0, 32),)),
        "output_grad": draw_output_grad(jax.random.fold_in(splits[7], 71), 0),
        "gate_act": scatter_about(splits[2], (TOKENS, FF), 2.0, 8.0, ((0, 32), (1, 8))),
        "down_weight": scatter_about(splits[3], (FF, D), D ** -0.5, 0.09375, ((0, 8), (1, 32))),
        "proj_in": scatter_about(splits[4], (K_IN, D), D ** -0.5, 0.09375),
        "proj_out": scatter_about(splits[5], (K_OUT, FF), FF ** -0.5, 0.046875, ((1, 8),)),
        "query": scatter_about(splits[6], (NQ, SK), 1.0, 6.0, ((0, 8), (1, 32))),
    }


def block_sketch(acts_blk, grad_blk, gate_blk, down_weight, proj_in, proj_out):
    hidden_grad = jnp.dot(grad_blk, down_weight.T, preferred_element_type=jnp.float32)
    up_grad = (hidden_grad * jax.nn.silu(gate_blk.astype(jnp.float32))).astype(jnp.bfloat16)
    in_proj = jnp.dot(proj_in, acts_blk.T, preferred_element_type=jnp.float32)
    out_proj = jnp.dot(proj_out, up_grad.T, preferred_element_type=jnp.float32)
    in_three = in_proj.reshape(K_IN, EX_DEV, SEQ)
    out_three = out_proj.reshape(K_OUT, EX_DEV, SEQ)
    sketch = jnp.einsum('iel,jel->eij', out_three, in_three, precision=lax.Precision.HIGHEST)
    return sketch.reshape(EX_DEV, K_OUT * K_IN).astype(jnp.bfloat16)

def reference(acts, output_grad, gate_act, down_weight, proj_in, proj_out, query):
    acts_blocks = acts.reshape(N_DP, TOK_DEV, D)
    grad_blocks = output_grad.reshape(N_DP, TOK_DEV, D)
    gate_blocks = gate_act.reshape(N_DP, TOK_DEV, FF)

    def one_block(items):
        return block_sketch(items[0], items[1], items[2], down_weight, proj_in, proj_out)
    sketches = lax.map(one_block, (acts_blocks, grad_blocks, gate_blocks)).reshape(EXAMPLES, SK)
    wide = sketches.astype(jnp.float32)
    trace = jnp.sum(wide * wide)
    raw_gram = jnp.dot(sketches.T, sketches, preferred_element_type=jnp.float32)
    gram = raw_gram * (SK / trace) + 0.1 * jnp.eye(SK, dtype=jnp.float32)
    raw_scores = jnp.dot(sketches, query.T, preferred_element_type=jnp.float32)
    scores = raw_scores / jnp.sqrt(trace / EXAMPLES)
    return (gram, scores)
```

```python
import jax
import jax.numpy as jnp
from jax import lax
from jax.experimental import pallas as pl
from jax.experimental.pallas import tpu as pltpu
from jax.sharding import PartitionSpec as P

SEQ = 256
SIDE = 4
LANES = 128
F_TILE = 256
LAST = (((1,), (1,)), ((), ()))


def dp_id(x, z, c):
    return ((x % SIDE) * SIDE + z % SIDE) * 2 + c


PLACES = [(x, z, c) for x in range(SIDE) for z in range(SIDE) for c in range(2)]
SAME_CORE = [[dp_id(x, z, c) for x in range(SIDE) for z in range(SIDE)] for c in range(2)]


def dp_move(value, where):
    return lax.ppermute(value, "dp", [(dp_id(*s), dp_id(*where(*s))) for s in PLACES])


def x_step(value):
    return dp_move(value, lambda x, z, c: (x + 1 - 2 * c, z, c))


def z_step(value):
    return dp_move(value, lambda x, z, c: (x, z + 1 - 2 * c, c))


def core_swap(value):
    return dp_move(value, lambda x, z, c: (x, z, 1 - c))


def tensor_swap(value, bit):
    return lax.ppermute(value, "tensor", [(t, t ^ bit) for t in range(8)])


def after(value, *others):
    return lax.optimization_barrier((value,) + others)[0]


def part_kernel(count, has_total, table, *refs):
    grads, weights, rest = refs[:count], refs[count:2 * count], refs[2 * count:]
    left = jnp.concatenate([g[...] for g in grads], axis=1)
    right = jnp.concatenate([w[...] for w in weights], axis=1)
    value = lax.dot_general(left, right, LAST, preferred_element_type=jnp.float32)
    if has_total:
        value = value + rest[0][...]
    rest[-1][...] = value


def grad_spec(rows, k):
    return pl.BlockSpec((rows, LANES), lambda f, table: (0, table[k]))


def add_part(table, grad, pieces, total):
    count = len(pieces)
    rows = grad.shape[0]
    hidden = 1792
    total_spec = pl.BlockSpec((rows, F_TILE), lambda f, table: (0, f))
    in_specs = [grad_spec(rows, k) for k in range(count)]
    in_specs += [pl.BlockSpec((F_TILE, LANES), lambda f, table: (f, 0))] * count
    args = [grad] * count + pieces
    if total is not None:
        in_specs.append(total_spec)
        args.append(total)
    return pl.pallas_call(
        lambda *refs: part_kernel(count, total is not None, *refs),
        out_shape=jax.ShapeDtypeStruct((rows, hidden), jnp.float32),
        grid_spec=pltpu.PrefetchScalarGridSpec(
            num_scalar_prefetch=1, grid=(hidden // F_TILE,), in_specs=in_specs, out_specs=total_spec
        ),
        cost_estimate=pl.CostEstimate(
            flops=2 * rows * hidden * LANES * count,
            bytes_accessed=count * (rows + hidden) * LANES * 2 + 8 * rows * hidden,
            transcendentals=0,
        ),
    )(table, *args)


def sketch_kernel(count, table, *refs):
    grads, weights = refs[:count], refs[count:2 * count]
    total, gate, proj_out, in_proj, out, out_side = refs[2 * count:]
    f = pl.program_id(0)
    left = jnp.concatenate([g[...] for g in grads], axis=1)
    right = jnp.concatenate([w[...] for w in weights], axis=1)
    hidden_grad = total[...] + lax.dot_general(left, right, LAST, preferred_element_type=jnp.float32)
    v = gate[...].astype(jnp.float32)
    up_grad = (hidden_grad * (v / (1.0 + jnp.exp(-v)))).astype(jnp.bfloat16)
    part = lax.dot_general(proj_out[...], up_grad, LAST, preferred_element_type=jnp.float32)

    @pl.when(f == 0)
    def _():
        out_side[...] = part

    @pl.when(f > 0)
    def _():
        out_side[...] += part

    @pl.when(f == pl.num_programs(0) - 1)
    def _():
        for e in range(2):
            tokens = pl.ds(e * SEQ, SEQ)
            sketch = lax.dot_general(
                out_side[:, tokens], in_proj[:, tokens], LAST,
                preferred_element_type=jnp.float32, precision=lax.Precision.HIGHEST,
            )
            out[e * 32:(e + 1) * 32, :] = jnp.concatenate([sketch[:32], sketch[32:]], axis=1)


def sketch_part(table, grad, pieces, total, gate, proj_out, in_proj):
    count = len(pieces)
    rows, hidden = gate.shape
    in_specs = [grad_spec(rows, k) for k in range(count)]
    in_specs += [pl.BlockSpec((F_TILE, LANES), lambda f, table: (f, 0))] * count
    in_specs += [
        pl.BlockSpec((rows, F_TILE), lambda f, table: (0, f)),
        pl.BlockSpec((rows, F_TILE), lambda f, table: (0, f)),
        pl.BlockSpec((64, F_TILE), lambda f, table: (0, f)),
        pl.BlockSpec((64, rows), lambda f, table: (0, 0)),
    ]
    return pl.pallas_call(
        lambda *refs: sketch_kernel(count, *refs),
        out_shape=jax.ShapeDtypeStruct((64, LANES), jnp.float32),
        grid_spec=pltpu.PrefetchScalarGridSpec(
            num_scalar_prefetch=1, grid=(hidden // F_TILE,), in_specs=in_specs,
            out_specs=pl.BlockSpec((64, LANES), lambda f, table: (0, 0)),
            scratch_shapes=[pltpu.VMEM((64, rows), jnp.float32)],
        ),
        cost_estimate=pl.CostEstimate(
            flops=2 * rows * hidden * (LANES * count + 64),
            bytes_accessed=count * (rows + hidden) * LANES * 2 + 6 * rows * hidden,
            transcendentals=rows * hidden,
        ),
    )(table, *([grad] * count), *pieces, total, gate, proj_out, in_proj)


def split3(value):
    high = value.astype(jnp.bfloat16)
    rest = value - high.astype(jnp.float32)
    mid = rest.astype(jnp.bfloat16)
    low = (rest - mid.astype(jnp.float32)).astype(jnp.bfloat16)
    return high, mid, low


def send_kernel(place, mine, other, queries, order, payload, raw_scores, wide, left):
    wide[...] = (mine[...] + other[...]).astype(jnp.bfloat16).astype(jnp.float32)
    whole = wide[...]
    squares = jnp.sum(jnp.sum(whole * whole, axis=0, keepdims=True), axis=1, keepdims=True)
    parts = [v.astype(jnp.float32) for v in split3(jnp.broadcast_to(squares, (1, LANES)))]
    tails = [[parts[0], parts[1]], [parts[2], jnp.zeros((1, LANES), jnp.float32)]]
    first_col = place[0] * 4
    cols = [[wide[pl.ds(e * 32 + first_col + r, 1), :] for r in range(4)] for e in range(2)]
    for p in range(16):
        rows = []
        for e in range(2):
            rows += cols[e] + [wide[e * 32 + 2 * p:e * 32 + 2 * p + 2, :]] + tails[e]
        payload[p] = jnp.concatenate(rows, axis=0).astype(jnp.bfloat16)
    left[...] = jnp.zeros_like(left)
    for k in range(32):
        for e in range(2):
            left[e:e + 1, k * LANES:(k + 1) * LANES] = wide[pl.ds(e * 32 + order[k], 1), :]
    raw_scores[...] = lax.dot_general(
        left[...].astype(jnp.bfloat16), queries[...], LAST, preferred_element_type=jnp.float32
    )


def send_part(place, mine, other, queries, order):
    smem, vmem = pl.BlockSpec(memory_space=pltpu.SMEM), pl.BlockSpec(memory_space=pltpu.VMEM)
    return pl.pallas_call(
        send_kernel,
        out_shape=(
            jax.ShapeDtypeStruct((16, 16, LANES), jnp.bfloat16),
            jax.ShapeDtypeStruct((8, LANES), jnp.float32),
        ),
        in_specs=[smem, vmem, vmem, vmem, smem],
        out_specs=(vmem, vmem),
        scratch_shapes=[pltpu.VMEM((64, LANES), jnp.float32), pltpu.VMEM((8, 4096), jnp.float32)],
    )(place, mine, other, queries, order)


def gram_kernel(place, mine, other, raw_scores, gram, scores):
    t, dp = place[0], place[1]
    odd = (dp % 2) == 1
    blocks = [mine[...].astype(jnp.float32), other[...].astype(jnp.float32)]

    def stack(r):
        return jnp.concatenate([b[:, e * 8 + r, :] for b in blocks for e in range(2)], axis=0)

    trace = jnp.zeros((1, LANES), jnp.float32)
    for b in blocks:
        for r in (15, 14, 7, 6):
            trace = trace + jnp.sum(b[:, r, :], axis=0, keepdims=True)
    row_part = jnp.where(odd, stack(5), stack(4)).astype(jnp.bfloat16)
    for r in range(4):
        raw = lax.dot_general(
            row_part, stack(r).astype(jnp.bfloat16), (((0,), (0,)), ((), ())),
            preferred_element_type=jnp.float32,
        )
        rows = dp * LANES + lax.broadcasted_iota(jnp.int32, raw.shape, 0)
        cols = t * 512 + r * LANES + lax.broadcasted_iota(jnp.int32, raw.shape, 1)
        gram[:, r * LANES:(r + 1) * LANES] = raw * (4096.0 / trace) + jnp.where(rows == cols, 0.1, 0.0)
    scores[...] = raw_scores[:2, :] / jnp.sqrt(trace / 64.0)


def gram_part(place, mine, other, raw_scores):
    smem, vmem = pl.BlockSpec(memory_space=pltpu.SMEM), pl.BlockSpec(memory_space=pltpu.VMEM)
    return pl.pallas_call(
        gram_kernel,
        out_shape=(
            jax.ShapeDtypeStruct((LANES, 512), jnp.float32),
            jax.ShapeDtypeStruct((2, LANES), jnp.float32),
        ),
        in_specs=[smem, vmem, vmem, vmem],
        out_specs=(vmem, vmem),
    )(place, mine, other, raw_scores)


def body(acts, output_grad, gate_act, down_weight, proj_in, proj_out, query):
    dp, tensor = lax.axis_index("dp"), lax.axis_index("tensor")
    x, z, c = dp // 8, (dp // 2) % SIDE, dp % 2
    sign = 1 - 2 * c
    hidden = down_weight.shape[0]

    block = jnp.concatenate([down_weight, query], axis=0)
    held = {(0, 0): block}
    for b in range(1, SIDE):
        held[0, b] = z_step(held[0, b - 1])
    sends = []
    for a, b in ((1, 0), (2, 0), (1, 1), (3, 0), (2, 1), (1, 2), (3, 1), (2, 2), (1, 3), (3, 2), (2, 3), (3, 3)):
        source = held[a - 1, b]
        if len(sends) >= 2:
            source = after(source, sends[-2])
        held[a, b] = x_step(source)
        sends.append(held[a, b])

    in_proj = lax.dot_general(proj_in, acts, LAST, preferred_element_type=jnp.float32)
    proj_out = jnp.concatenate([proj_out.reshape(32, 2, hidden)[:, k] for k in range(2)], axis=0)

    groups = [[(a, b) for a in range(SIDE)] for b in range(SIDE)]
    groups[-1].remove((3, 3))
    groups.append([(3, 3)])
    total, query_parts, order = None, [], []
    for group in groups:
        own = [held[key] for key in group]
        pieces = own + [core_swap(piece) for piece in own]
        table = jnp.stack(
            [dp_id(x - sign * a, z - sign * b, c) for a, b in group]
            + [dp_id(x + sign * a, z + sign * b, 1 - c) for a, b in group]
        ).astype(jnp.int32)
        order.append(table)
        query_parts += [piece[hidden:] for piece in pieces]
        if group is groups[-1]:
            sketch = sketch_part(table, output_grad, pieces, total, gate_act, proj_out, in_proj)
        else:
            total = add_part(table, output_grad, pieces, total)
    queries = jnp.concatenate(query_parts, axis=1)
    order = jnp.concatenate(order)

    sketch = sketch + tensor_swap(sketch, 4)
    sketch = sketch + tensor_swap(sketch, 1)
    place = jnp.stack([tensor, dp]).astype(jnp.int32)
    payload, raw_scores = send_part(place, sketch, tensor_swap(sketch, 2), queries, order)
    mine = lax.all_to_all(payload, "dp", 0, 0, axis_index_groups=SAME_CORE)
    return gram_part(place, mine, core_swap(mine), raw_scores)


def solution(mesh):
    placed = (
        P("dp", None),
        P("dp", None),
        P("dp", "tensor"),
        P("tensor", "dp"),
        P(),
        P(None, "tensor"),
        P("tensor", "dp"),
    )
    return jax.shard_map(
        body,
        mesh=mesh,
        in_specs=placed,
        out_specs=(P("dp", "tensor"), P("dp", "tensor")),
        check_vma=False,
    )
```

```python
import jax
import jax.numpy as jnp
from jax import lax
from jax.experimental import pallas as pl
from jax.experimental.pallas import tpu as pltpu
from jax.sharding import PartitionSpec as P

SEQ = 256
SIDE = 4
LANES = 128
HALF = 896
VMEM_BYTES = 56 << 20
LAST = (((1,), (1,)), ((), ()))


def dp_id(x, z, c):
    return ((x % SIDE) * SIDE + z % SIDE) * 2 + c


PLACES = [(x, z, c) for x in range(SIDE) for z in range(SIDE) for c in range(2)]
SAME_CORE = [[dp_id(x, z, c) for x in range(SIDE) for z in range(SIDE)] for c in range(2)]


FROM = (0, -1, 1, -2)
X_ORDER = [
    (1, 0), (2, 0), (3, 0), (1, 1), (2, 1), (1, 2), (2, 2), (3, 1), (1, 3), (3, 2), (2, 3), (3, 3),
]
IN_FLIGHT = 3
ARRIVAL = [(0, 0), (0, 1), (0, 2), (1, 0), (2, 0), (3, 0), (1, 1), (2, 1), (1, 2), (2, 2), (3, 1), (0, 3)]
ARRIVAL += [(1, 3), (3, 2), (2, 3), (3, 3)]


def dp_move(value, where):
    return lax.ppermute(value, "dp", [(dp_id(*s), dp_id(*where(*s))) for s in PLACES])


def x_step(value, way):
    return dp_move(value, lambda x, z, c: (x + way * (1 - 2 * c), z, c))


def z_step(value, way):
    return dp_move(value, lambda x, z, c: (x, z + way * (1 - 2 * c), c))


def core_swap(value):
    return dp_move(value, lambda x, z, c: (x, z, 1 - c))


def tensor_swap(value, bit):
    return lax.ppermute(value, "tensor", [(t, t ^ bit) for t in range(8)])


def after(value, *others):
    return lax.optimization_barrier((value,) + others)[0]


def piece_copies(table, grads, pieces, first, weight, grad, queries, sem):
    made = []
    for p, piece in enumerate(pieces):
        k = first + 2 * p
        made.append((piece.at[:, :HALF], weight.at[k:k + 2]))
        made.append((piece.at[:, HALF:], queries.at[k:k + 2]))
    for k in range(first, first + 2 * len(pieces)):
        span = pl.ds(pl.multiple_of(table[k] * LANES, LANES), LANES)
        made += [(grads[side].at[:, span], grad.at[side, k]) for side in range(2)]
    return [pltpu.make_async_copy(x, y, sem) for x, y in made]


def start(copies):
    for copy in copies:
        copy.start()


def finish(copies):
    for copy in copies:
        copy.wait()


def product(weight, grad, span, e):
    left = jnp.concatenate([weight[k] for k in span], axis=1)
    rows = slice((e % 2) * SEQ, (e % 2 + 1) * SEQ)
    right = jnp.concatenate([grad[e // 2, k, rows, :] for k in span], axis=1)
    return lax.dot_general(left, right, LAST, preferred_element_type=jnp.float32)


def early_kernel(count, table, *refs):
    grads, pieces = refs[:2], refs[2:2 + count]
    out, queries, weight, grad, total, sems, out_sem = refs[2 + count:]
    groups = count // SIDE
    moving = [
        piece_copies(
            table, grads, pieces[SIDE * b:SIDE * b + SIDE], 2 * SIDE * b, weight, grad, queries, sems.at[b]
        )
        for b in range(groups)
    ]
    start(moving[0])
    start(moving[1])
    for b in range(groups):
        finish(moving[b])
        if b + 2 < groups:
            start(moving[b + 2])

        @pl.when(table[0] >= 0)
        def _():
            for e in range(4):
                value = product(weight, grad, range(2 * SIDE * b, 2 * SIDE * (b + 1)), e)
                total[e] = value if b == 0 else value + total[e]
    write = pltpu.make_async_copy(total, out, out_sem)
    write.start()
    write.wait()


def late_kernel(count, table, *refs):
    grads, pieces = refs[:2], refs[2:2 + count]
    held, gate_own, gate_other, proj_out, in_own, in_other = refs[2 + count:8 + count]
    out_own, out_other, queries, weight, grad, total, value, gate, sem, total_sem = refs[8 + count:]
    moving = piece_copies(table, grads, pieces, 0, weight, grad, queries, sem)
    later = [pltpu.make_async_copy(held, total, total_sem)]
    later += [pltpu.make_async_copy(ref, gate.at[n], total_sem) for n, ref in enumerate((gate_own, gate_other))]
    start(moving)
    start(later)
    finish(moving)

    @pl.when(table[0] >= 0)
    def _():
        for e in range(4):
            value[e] = product(weight, grad, range(2 * count), e)

    finish(later)
    sides = []
    for e in range(4):
        v = gate[e // 2, :, (e % 2) * SEQ:(e % 2 + 1) * SEQ].astype(jnp.float32)
        up_grad = ((value[e] + total[e]) * (v / (1.0 + jnp.exp(-v)))).astype(jnp.bfloat16)
        sides.append(jnp.dot(proj_out[...], up_grad, preferred_element_type=jnp.float32))
    for e, out_side in enumerate(sides):
        in_side = (in_own, in_other)[e // 2][:, (e % 2) * SEQ:(e % 2 + 1) * SEQ]
        sketch = lax.dot_general(
            out_side, in_side, LAST, preferred_element_type=jnp.float32, precision=lax.Precision.HIGHEST
        )
        out = (out_own, out_other)[e // 2]
        out[(e % 2) * 32:(e % 2 + 1) * 32, :] = jnp.concatenate([sketch[:32], sketch[32:]], axis=1)


def grad_part(table, grads, pieces, tail=None):
    count = len(pieces)
    rows = grads[0].shape[0]
    smem, vmem, anywhere = [pl.BlockSpec(memory_space=m) for m in (pltpu.SMEM, pltpu.VMEM, pl.ANY)]
    total = ((4, HALF, SEQ), jnp.float32)
    queries = jax.ShapeDtypeStruct((2 * count, 64, LANES), jnp.bfloat16)
    scratch = [
        pltpu.VMEM((2 * count, HALF, LANES), jnp.bfloat16),
        pltpu.VMEM((2, 2 * count, rows, LANES), jnp.bfloat16),
        pltpu.VMEM(*total),
    ]
    if tail:
        kernel = late_kernel
        shapes, out_specs = [jax.ShapeDtypeStruct((64, LANES), jnp.float32)] * 2, [vmem] * 3
        in_specs = [anywhere] * (5 + count) + [vmem] * 3
        scratch += [pltpu.VMEM(*total), pltpu.VMEM((2, HALF, rows), jnp.bfloat16)]
        scratch += [pltpu.SemaphoreType.DMA, pltpu.SemaphoreType.DMA]
    else:
        kernel = early_kernel
        shapes, out_specs = [jax.ShapeDtypeStruct(*total)], [anywhere, vmem]
        in_specs = [anywhere] * (2 + count)
        scratch += [pltpu.SemaphoreType.DMA((count // SIDE,)), pltpu.SemaphoreType.DMA]
    return pl.pallas_call(
        lambda *refs: kernel(count, *refs),
        out_shape=shapes + [queries],
        in_specs=[smem] + in_specs,
        out_specs=out_specs,
        scratch_shapes=scratch,
        compiler_params=pltpu.CompilerParams(vmem_limit_bytes=VMEM_BYTES),
        cost_estimate=pl.CostEstimate(
            flops=8 * rows * HALF * count * LANES, bytes_accessed=count << 20, transcendentals=0
        ),
    )(table, *grads, *pieces, *(tail or ()))


def split3(value):
    high = value.astype(jnp.bfloat16)
    rest = value - high.astype(jnp.float32)
    mid = rest.astype(jnp.bfloat16)
    low = (rest - mid.astype(jnp.float32)).astype(jnp.bfloat16)
    return high, mid, low


def send_kernel(parts_count, place, order, parts, *refs):
    own_queries, other_queries = refs[:parts_count], refs[parts_count:2 * parts_count]
    payload, raw_scores, wide, left = refs[2 * parts_count:]
    sketch = parts[0]
    for k in range(1, 8):
        sketch = sketch + parts[k]
    wide[...] = sketch.astype(jnp.bfloat16).astype(jnp.float32)
    whole = wide[...]
    squares = jnp.sum(jnp.sum(whole * whole, axis=0, keepdims=True), axis=1, keepdims=True)
    parts = [v.astype(jnp.float32) for v in split3(jnp.broadcast_to(squares, (1, LANES)))]
    tails = [[parts[0], parts[1]], [parts[2], jnp.zeros((1, LANES), jnp.float32)]]
    first_col = place[0] * 4
    cols = [[wide[pl.ds(e * 32 + first_col + r, 1), :] for r in range(4)] for e in range(2)]
    for p in range(16):
        rows = []
        for e in range(2):
            rows += cols[e] + [wide[e * 32 + 2 * p:e * 32 + 2 * p + 2, :]] + tails[e]
        payload[p] = jnp.concatenate(rows, axis=0).astype(jnp.bfloat16)
    left[...] = jnp.zeros_like(left)
    raw = []
    for q, queries in enumerate((own_queries, other_queries)):
        for k in range(32):
            for e in range(2):
                left[e:e + 1, k * LANES:(k + 1) * LANES] = wide[pl.ds(e * 32 + order[q * 32 + k], 1), :]
        right = jnp.concatenate([part[k] for part in queries for k in range(part.shape[0])], axis=1)
        raw.append(lax.dot_general(
            left[...].astype(jnp.bfloat16), right, LAST, preferred_element_type=jnp.float32
        ))
    even = (place[1] % 2) == 0
    raw_scores[...] = jnp.where(
        even, jnp.concatenate(raw, axis=1), jnp.concatenate(raw[::-1], axis=1)
    )


def send_part(place, sketches, own_queries, other_queries, order):
    smem, vmem = pl.BlockSpec(memory_space=pltpu.SMEM), pl.BlockSpec(memory_space=pltpu.VMEM)
    return pl.pallas_call(
        lambda *refs: send_kernel(len(own_queries), *refs),
        out_shape=(
            jax.ShapeDtypeStruct((16, 16, LANES), jnp.bfloat16),
            jax.ShapeDtypeStruct((8, LANES), jnp.float32),
        ),
        in_specs=[smem, smem] + [vmem] * (1 + 2 * len(own_queries)),
        out_specs=(vmem, vmem),
        scratch_shapes=[pltpu.VMEM((64, LANES), jnp.float32), pltpu.VMEM((8, 4096), jnp.float32)],
    )(place, order, sketches, *own_queries, *other_queries)


def gram_kernel(place, mine, other, raw_scores, gram, scores):
    t, dp = place[0], place[1]
    odd = (dp % 2) == 1
    blocks = [mine[...].astype(jnp.float32), other[...].astype(jnp.float32)]

    def stack(r):
        return jnp.concatenate([b[:, e * 8 + r, :] for b in blocks for e in range(2)], axis=0)

    trace = jnp.zeros((1, LANES), jnp.float32)
    for b in blocks:
        for r in (15, 14, 7, 6):
            trace = trace + jnp.sum(b[:, r, :], axis=0, keepdims=True)
    row_part = jnp.where(odd, stack(5), stack(4)).astype(jnp.bfloat16)
    for r in range(4):
        raw = lax.dot_general(
            row_part, stack(r).astype(jnp.bfloat16), (((0,), (0,)), ((), ())),
            preferred_element_type=jnp.float32,
        )
        rows = dp * LANES + lax.broadcasted_iota(jnp.int32, raw.shape, 0)
        cols = t * 512 + r * LANES + lax.broadcasted_iota(jnp.int32, raw.shape, 1)
        gram[:, r * LANES:(r + 1) * LANES] = raw * (4096.0 / trace) + jnp.where(rows == cols, 0.1, 0.0)
    scores[...] = raw_scores[:2, :] / jnp.sqrt(trace / 64.0)


def gram_part(place, mine, other, raw_scores):
    smem, vmem = pl.BlockSpec(memory_space=pltpu.SMEM), pl.BlockSpec(memory_space=pltpu.VMEM)
    return pl.pallas_call(
        gram_kernel,
        out_shape=(
            jax.ShapeDtypeStruct((LANES, 512), jnp.float32),
            jax.ShapeDtypeStruct((2, LANES), jnp.float32),
        ),
        in_specs=[smem, vmem, vmem, vmem],
        out_specs=(vmem, vmem),
    )(place, mine, other, raw_scores)


def halves(value, c, axis):
    size = value.shape[axis] // 2
    return [lax.dynamic_slice_in_dim(value, h * size, size, axis) for h in (c, 1 - c)]


def gather_pieces(down_weight, query, c):
    pair = (down_weight, query)
    first = jnp.stack([
        jnp.concatenate([halves(v, c, 0)[0] for v in values])
        for values in (pair, [core_swap(v) for v in pair])
    ])
    held = {(0, 0): first}
    held[0, 1], held[0, 2] = z_step(first, 1), z_step(first, -1)
    held[0, 3] = z_step(held[0, 1], 1)
    for n, (a, b) in enumerate(X_ORDER):
        source = held[1 if a == 3 else 0, b]
        if n >= IN_FLIGHT:
            source = after(source, held[X_ORDER[n - IN_FLIGHT]])
        held[a, b] = x_step(source, -1 if a == 2 else 1)
    return held


def body(acts, output_grad, gate_act, down_weight, proj_in, proj_out, query):
    dp, tensor = lax.axis_index("dp"), lax.axis_index("tensor")
    x, z, c = dp // 8, (dp // 2) % SIDE, dp % 2
    hidden = down_weight.shape[0]

    held = gather_pieces(down_weight, query, c)
    grads = (output_grad, core_swap(after(output_grad, held[0, 0])))
    gate_keep, gate_give = halves(gate_act, c, 1)
    gates = (gate_keep.T, core_swap(after(gate_give, held[0, 0])).T)
    in_proj = lax.dot_general(proj_in, acts, LAST, preferred_element_type=jnp.float32)
    in_projs = (in_proj, core_swap(in_proj))
    proj_half = halves(proj_out, c, 1)[0].reshape(32, 2, hidden // 2)
    proj_half = jnp.concatenate([proj_half[:, k] for k in range(2)], axis=0)

    def columns(keys, core):
        sign = 1 - 2 * core
        return jnp.stack([
            dp_id(x + sign * FROM[a], z + sign * FROM[b], k) for a, b in keys for k in (core, 1 - core)
        ]).astype(jnp.int32)

    early, late = ARRIVAL[:12], ARRIVAL[12:]
    total, early_queries = grad_part(columns(early, c), grads, [held[key] for key in early])
    own_part, other_part, late_queries = grad_part(
        columns(late, c), grads, [held[key] for key in late], (total, *gates, proj_half, *in_projs)
    )
    own_queries = [early_queries, late_queries]
    other_queries = [core_swap(part) for part in own_queries]
    order = jnp.concatenate([columns(ARRIVAL, c), columns(ARRIVAL, 1 - c)])
    sketch = own_part + core_swap(other_part)
    sketches = lax.all_to_all(jnp.broadcast_to(sketch[None], (8,) + sketch.shape), "tensor", 0, 0)
    place = jnp.stack([tensor, dp]).astype(jnp.int32)
    payload, raw_scores = send_part(place, sketches, own_queries, other_queries, order)
    mine = lax.all_to_all(payload, "dp", 0, 0, axis_index_groups=SAME_CORE)
    return gram_part(place, mine, core_swap(mine), raw_scores)


def solution(mesh):
    placed = (
        P("dp", None),
        P("dp", None),
        P("dp", "tensor"),
        P("tensor", "dp"),
        P(),
        P(None, "tensor"),
        P("tensor", "dp"),
    )
    return jax.shard_map(
        body,
        mesh=mesh,
        in_specs=placed,
        out_specs=(P("dp", "tensor"), P("dp", "tensor")),
        check_vma=False,
    )
```

```python
import jax
import jax.numpy as jnp
from jax import lax
from jax.experimental import pallas as pl
from jax.experimental.pallas import tpu as pltpu
from jax.sharding import PartitionSpec as P

SEQ = 256
SIDE = 4
LANES = 128
HALF = 896
VMEM_BYTES = 56 << 20
LAST = (((1,), (1,)), ((), ()))


def dp_id(x, z, c):
    return ((x % SIDE) * SIDE + z % SIDE) * 2 + c


PLACES = [(x, z, c) for x in range(SIDE) for z in range(SIDE) for c in range(2)]


FROM = (0, -1, 1, -2)
X_ORDER = [
    (1, 0), (2, 0), (3, 0), (1, 1), (2, 1), (1, 2), (2, 2), (3, 1), (1, 3), (2, 3), (3, 3),
]
IN_FLIGHT = 3
ARRIVAL = [(0, 0), (0, 1), (0, 2), (1, 0), (2, 0), (3, 0), (1, 1), (2, 1), (1, 2), (2, 2), (3, 1), (0, 3)]
ARRIVAL += [(1, 3), (3, 2), (2, 3), (3, 3)]


def dp_move(value, where):
    return lax.ppermute(value, "dp", [(dp_id(*s), dp_id(*where(*s))) for s in PLACES])


def x_step(value, way):
    return dp_move(value, lambda x, z, c: (x + way * (1 - 2 * c), z, c))


def z_step(value, way):
    return dp_move(value, lambda x, z, c: (x, z + way * (1 - 2 * c), c))


def core_swap(value):
    return dp_move(value, lambda x, z, c: (x, z, 1 - c))


def tensor_swap(value, bit):
    return lax.ppermute(value, "tensor", [(t, t ^ bit) for t in range(8)])


def after(value, *others):
    return lax.optimization_barrier((value,) + others)[0]


def piece_copies(table, grads, pieces, first, weight, grad, queries, sem):
    made = []
    for p, piece in enumerate(pieces):
        k = first + 2 * p
        made.append((piece.at[:, :HALF], weight.at[k:k + 2]))
        made.append((piece.at[:, HALF:], queries.at[k:k + 2]))
    for k in range(first, first + 2 * len(pieces)):
        span = pl.ds(pl.multiple_of(table[k] * LANES, LANES), LANES)
        made += [(grads[side].at[:, span], grad.at[side, k]) for side in range(2)]
    return [pltpu.make_async_copy(x, y, sem) for x, y in made]


def start(copies):
    for copy in copies:
        copy.start()


def finish(copies):
    for copy in copies:
        copy.wait()


def product(weight, grad, span, e):
    left = jnp.concatenate([weight[k] for k in span], axis=1)
    rows = slice((e % 2) * SEQ, (e % 2 + 1) * SEQ)
    right = jnp.concatenate([grad[e // 2, k, rows, :] for k in span], axis=1)
    return lax.dot_general(left, right, LAST, preferred_element_type=jnp.float32)


def early_kernel(count, table, *refs):
    grads, pieces = refs[:2], refs[2:2 + count]
    out, queries, weight, grad, total, sems, out_sem = refs[2 + count:]
    groups = count // SIDE
    moving = [
        piece_copies(
            table, grads, pieces[SIDE * b:SIDE * b + SIDE], 2 * SIDE * b, weight, grad, queries, sems.at[b]
        )
        for b in range(groups)
    ]
    start(moving[0])
    start(moving[1])
    for b in range(groups):
        finish(moving[b])
        if b + 2 < groups:
            start(moving[b + 2])

        @pl.when(table[0] >= 0)
        def _():
            for e in range(4):
                value = product(weight, grad, range(2 * SIDE * b, 2 * SIDE * (b + 1)), e)
                total[e] = value if b == 0 else value + total[e]
    write = pltpu.make_async_copy(total, out, out_sem)
    write.start()
    write.wait()


def late_kernel(count, table, *refs):
    grads, pieces = refs[:2], refs[2:2 + count]
    held, gate_own, gate_other, proj_out, in_own, in_other = refs[2 + count:8 + count]
    out_own, out_other, queries, weight, grad, total, value, gate, sem, total_sem = refs[8 + count:]
    moving = piece_copies(table, grads, pieces, 0, weight, grad, queries, sem)
    later = [pltpu.make_async_copy(held, total, total_sem)]
    later += [pltpu.make_async_copy(ref, gate.at[n], total_sem) for n, ref in enumerate((gate_own, gate_other))]
    start(moving)
    start(later)
    finish(moving)

    @pl.when(table[0] >= 0)
    def _():
        for e in range(4):
            value[e] = product(weight, grad, range(2 * count), e)

    finish(later)
    sides = []
    for e in range(4):
        v = gate[e // 2, :, (e % 2) * SEQ:(e % 2 + 1) * SEQ].astype(jnp.float32)
        up_grad = ((value[e] + total[e]) * (v / (1.0 + jnp.exp(-v)))).astype(jnp.bfloat16)
        sides.append(jnp.dot(proj_out[...], up_grad, preferred_element_type=jnp.float32))
    for e, out_side in enumerate(sides):
        in_side = (in_own, in_other)[e // 2][:, (e % 2) * SEQ:(e % 2 + 1) * SEQ]
        sketch = lax.dot_general(
            out_side, in_side, LAST, preferred_element_type=jnp.float32, precision=lax.Precision.HIGHEST
        )
        out = (out_own, out_other)[e // 2]
        out[(e % 2) * 32:(e % 2 + 1) * 32, :] = jnp.concatenate([sketch[:32], sketch[32:]], axis=1)


def grad_part(table, grads, pieces, tail=None):
    count = len(pieces)
    rows = grads[0].shape[0]
    smem, vmem, anywhere = [pl.BlockSpec(memory_space=m) for m in (pltpu.SMEM, pltpu.VMEM, pl.ANY)]
    total = ((4, HALF, SEQ), jnp.float32)
    queries = jax.ShapeDtypeStruct((2 * count, 64, LANES), jnp.bfloat16)
    scratch = [
        pltpu.VMEM((2 * count, HALF, LANES), jnp.bfloat16),
        pltpu.VMEM((2, 2 * count, rows, LANES), jnp.bfloat16),
        pltpu.VMEM(*total),
    ]
    if tail:
        kernel = late_kernel
        shapes, out_specs = [jax.ShapeDtypeStruct((64, LANES), jnp.float32)] * 2, [vmem] * 3
        in_specs = [anywhere] * (5 + count) + [vmem] * 3
        scratch += [pltpu.VMEM(*total), pltpu.VMEM((2, HALF, rows), jnp.bfloat16)]
        scratch += [pltpu.SemaphoreType.DMA, pltpu.SemaphoreType.DMA]
    else:
        kernel = early_kernel
        shapes, out_specs = [jax.ShapeDtypeStruct(*total)], [anywhere, vmem]
        in_specs = [anywhere] * (2 + count)
        scratch += [pltpu.SemaphoreType.DMA((count // SIDE,)), pltpu.SemaphoreType.DMA]
    return pl.pallas_call(
        lambda *refs: kernel(count, *refs),
        out_shape=shapes + [queries],
        in_specs=[smem] + in_specs,
        out_specs=out_specs,
        scratch_shapes=scratch,
        compiler_params=pltpu.CompilerParams(vmem_limit_bytes=VMEM_BYTES),
        cost_estimate=pl.CostEstimate(
            flops=8 * rows * HALF * count * LANES, bytes_accessed=count << 20, transcendentals=0
        ),
    )(table, *grads, *pieces, *(tail or ()))


def split3(value):
    high = value.astype(jnp.bfloat16)
    rest = value - high.astype(jnp.float32)
    mid = rest.astype(jnp.bfloat16)
    low = (rest - mid.astype(jnp.float32)).astype(jnp.bfloat16)
    return high, mid, low


def send_kernel(place, parts, payload, wide):
    sketch = parts[0]
    for k in range(1, 8):
        sketch = sketch + parts[k]
    wide[...] = sketch.astype(jnp.bfloat16).astype(jnp.float32)
    whole = wide[...]
    squares = jnp.sum(jnp.sum(whole * whole, axis=0, keepdims=True), axis=1, keepdims=True)
    parts = [v.astype(jnp.float32) for v in split3(jnp.broadcast_to(squares, (1, LANES)))]
    zero = jnp.zeros((1, LANES), jnp.float32)
    tails = [parts, [zero] * 3]
    first_col = place[0] * 4
    cols = [[wide[pl.ds(e * 32 + first_col + r, 1), :] for r in range(4)] for e in range(2)]
    for p in range(32):
        rows = []
        for e in range(2):
            rows += cols[e] + [wide[e * 32 + p:e * 32 + p + 1, :]] + tails[e]
        payload[p] = jnp.concatenate(rows, axis=0).astype(jnp.bfloat16)


def scores_kernel(count, place, order, wide, *refs):
    own_queries, other_queries = refs[:count], refs[count:2 * count]
    raw_scores, left = refs[2 * count:]
    left[...] = jnp.zeros_like(left)
    raw = []
    for q, queries in enumerate((own_queries, other_queries)):
        for k in range(32):
            for e in range(2):
                left[e:e + 1, k * LANES:(k + 1) * LANES] = wide[pl.ds(e * 32 + order[q * 32 + k], 1), :]
        right = jnp.concatenate([part[k] for part in queries for k in range(part.shape[0])], axis=1)
        raw.append(lax.dot_general(
            left[...].astype(jnp.bfloat16), right, LAST, preferred_element_type=jnp.float32
        ))
    even = (place[1] % 2) == 0
    raw_scores[...] = jnp.where(
        even, jnp.concatenate(raw, axis=1), jnp.concatenate(raw[::-1], axis=1)
    )


def send_part(place, sketches):
    smem, vmem = pl.BlockSpec(memory_space=pltpu.SMEM), pl.BlockSpec(memory_space=pltpu.VMEM)
    return pl.pallas_call(
        send_kernel,
        out_shape=(
            jax.ShapeDtypeStruct((32, 16, LANES), jnp.bfloat16),
            jax.ShapeDtypeStruct((64, LANES), jnp.float32),
        ),
        in_specs=[smem, vmem],
        out_specs=(vmem, vmem),
    )(place, sketches)


def scores_part(place, order, wide, own_queries, other_queries):
    smem, vmem = pl.BlockSpec(memory_space=pltpu.SMEM), pl.BlockSpec(memory_space=pltpu.VMEM)
    return pl.pallas_call(
        lambda *refs: scores_kernel(len(own_queries), *refs),
        out_shape=jax.ShapeDtypeStruct((8, LANES), jnp.float32),
        in_specs=[smem, smem] + [vmem] * (1 + 2 * len(own_queries)),
        out_specs=vmem,
        scratch_shapes=[pltpu.VMEM((8, 4096), jnp.float32)],
        cost_estimate=pl.CostEstimate(flops=2 * 8 * 4096 * 128, bytes_accessed=2 << 20, transcendentals=0),
    )(place, order, wide, *own_queries, *other_queries)


def gram_kernel(place, mine, raw_scores, gram, scores):
    t, dp = place[0], place[1]
    wide = mine[...].astype(jnp.float32)

    def stack(r):
        return jnp.concatenate([wide[:, r, :], wide[:, 8 + r, :]], axis=0).astype(jnp.bfloat16)

    trace = jnp.zeros((1, LANES), jnp.float32)
    for r in (7, 6, 5):
        trace = trace + jnp.sum(wide[:, r, :], axis=0, keepdims=True)
    row_part = stack(4)
    for r in range(4):
        raw = lax.dot_general(
            row_part, stack(r), (((0,), (0,)), ((), ())),
            preferred_element_type=jnp.float32,
        )
        rows = dp * LANES + lax.broadcasted_iota(jnp.int32, raw.shape, 0)
        cols = t * 512 + r * LANES + lax.broadcasted_iota(jnp.int32, raw.shape, 1)
        gram[:, r * LANES:(r + 1) * LANES] = raw * (4096.0 / trace) + jnp.where(rows == cols, 0.1, 0.0)
    scores[...] = raw_scores[:2, :] / jnp.sqrt(trace / 64.0)


def gram_part(place, mine, raw_scores):
    smem, vmem = pl.BlockSpec(memory_space=pltpu.SMEM), pl.BlockSpec(memory_space=pltpu.VMEM)
    return pl.pallas_call(
        gram_kernel,
        out_shape=(
            jax.ShapeDtypeStruct((LANES, 512), jnp.float32),
            jax.ShapeDtypeStruct((2, LANES), jnp.float32),
        ),
        in_specs=[smem, vmem, vmem],
        out_specs=(vmem, vmem),
    )(place, mine, raw_scores)


def halves(value, c, axis):
    size = value.shape[axis] // 2
    return [lax.dynamic_slice_in_dim(value, h * size, size, axis) for h in (c, 1 - c)]


def gather_pieces(down_weight, query, c):
    pair = (down_weight, query)
    first = jnp.stack([
        jnp.concatenate([halves(v, c, 0)[0] for v in values])
        for values in (pair, [core_swap(v) for v in pair])
    ])
    held = {(0, 0): first}
    held[0, 1], held[0, 2] = z_step(first, 1), z_step(first, -1)
    held[0, 3] = z_step(held[0, 1], 1)
    for n, (a, b) in enumerate(X_ORDER):
        source = held[1 if a == 3 else 0, b]
        if n >= IN_FLIGHT:
            source = after(source, held[X_ORDER[n - IN_FLIGHT]])
        held[a, b] = x_step(source, -1 if a == 2 else 1)
        if (a, b) == (3, 0):
            held[3, 2] = z_step(after(held[3, 0], held[0, 3]), -1)
    return held


def body(acts, output_grad, gate_act, down_weight, proj_in, proj_out, query):
    dp, tensor = lax.axis_index("dp"), lax.axis_index("tensor")
    x, z, c = dp // 8, (dp // 2) % SIDE, dp % 2
    hidden = down_weight.shape[0]

    held = gather_pieces(down_weight, query, c)
    grads = (output_grad, core_swap(after(output_grad, held[0, 0])))
    gate_keep, gate_give = halves(gate_act, c, 1)
    gates = (gate_keep.T, core_swap(after(gate_give, held[0, 0])).T)
    in_proj = lax.dot_general(proj_in, acts, LAST, preferred_element_type=jnp.float32)
    in_projs = (in_proj, core_swap(in_proj))
    proj_half = halves(proj_out, c, 1)[0].reshape(32, 2, hidden // 2)
    proj_half = jnp.concatenate([proj_half[:, k] for k in range(2)], axis=0)

    def columns(keys, core):
        sign = 1 - 2 * core
        return jnp.stack([
            dp_id(x + sign * FROM[a], z + sign * FROM[b], k) for a, b in keys for k in (core, 1 - core)
        ]).astype(jnp.int32)

    early, late = ARRIVAL[:12], ARRIVAL[12:]
    total, early_queries = grad_part(columns(early, c), grads, [held[key] for key in early])
    own_part, other_part, late_queries = grad_part(
        columns(late, c), grads, [held[key] for key in late], (total, *gates, proj_half, *in_projs)
    )
    own_queries = [early_queries, late_queries]
    other_queries = [core_swap(part) for part in own_queries]
    order = jnp.concatenate([columns(ARRIVAL, c), columns(ARRIVAL, 1 - c)])
    eight = lax.optimization_barrier(jnp.broadcast_to(own_part[None], (8,) + own_part.shape))
    sketches = lax.all_to_all(eight + core_swap(other_part)[None], "tensor", 0, 0)
    place = jnp.stack([tensor, dp]).astype(jnp.int32)
    payload, wide = send_part(place, sketches)
    mine = lax.all_to_all(payload, "dp", 0, 0)
    raw_scores = scores_part(place, order, wide, own_queries, other_queries)
    return gram_part(place, mine, raw_scores)


def solution(mesh):
    placed = (
        P("dp", None),
        P("dp", None),
        P("dp", "tensor"),
        P("tensor", "dp"),
        P(),
        P(None, "tensor"),
        P("tensor", "dp"),
    )
    return jax.shard_map(
        body,
        mesh=mesh,
        in_specs=placed,
        out_specs=(P("dp", "tensor"), P("dp", "tensor")),
        check_vma=False,
    )
```

```python
import jax
import jax.numpy as jnp
from jax import lax
from jax.experimental import pallas as pl
from jax.experimental.pallas import tpu as pltpu
from jax.sharding import PartitionSpec as P

SEQ = 256
SIDE = 4
LANES = 128
HALF = 896
VMEM_BYTES = 36 << 20
LAST = (((1,), (1,)), ((), ()))


def dp_id(x, z, c):
    return ((x % SIDE) * SIDE + z % SIDE) * 2 + c


PLACES = [(x, z, c) for x in range(SIDE) for z in range(SIDE) for c in range(2)]


FROM = (0, -1, 1, -2)
X_ORDER = [
    (1, 0), (2, 0), (3, 0), (1, 1), (2, 1), (1, 2), (2, 2), (3, 1), (1, 3), (2, 3), (3, 3),
]
IN_FLIGHT = 3
ARRIVAL = [(0, 0), (0, 1), (0, 2), (1, 0), (2, 0), (3, 0), (1, 1), (2, 1), (1, 2), (2, 2), (3, 1), (0, 3)]
ARRIVAL += [(1, 3), (3, 2), (2, 3), (3, 3)]


def dp_move(value, where):
    return lax.ppermute(value, "dp", [(dp_id(*s), dp_id(*where(*s))) for s in PLACES])


def x_step(value, way):
    return dp_move(value, lambda x, z, c: (x + way * (1 - 2 * c), z, c))


def z_step(value, way):
    return dp_move(value, lambda x, z, c: (x, z + way * (1 - 2 * c), c))


def core_swap(value):
    return dp_move(value, lambda x, z, c: (x, z, 1 - c))


def tensor_swap(value, bit):
    return lax.ppermute(value, "tensor", [(t, t ^ bit) for t in range(8)])


def after(value, *others):
    return lax.optimization_barrier((value,) + others)[0]


def piece_copies(table, grads, pieces, first, weight, grad, queries, sem):
    made = []
    for p, piece in enumerate(pieces):
        k = first + 2 * p
        made.append((piece.at[:, :HALF], weight.at[k:k + 2]))
        made.append((piece.at[:, HALF:], queries.at[k:k + 2]))
    for k in range(first, first + 2 * len(pieces)):
        span = pl.ds(pl.multiple_of(table[k] * LANES, LANES), LANES)
        made += [(grads[side].at[:, span], grad.at[side, k]) for side in range(2)]
    return [pltpu.make_async_copy(x, y, sem) for x, y in made]


def start(copies):
    for copy in copies:
        copy.start()


def finish(copies):
    for copy in copies:
        copy.wait()


def product(weight, grad, span, e):
    left = jnp.concatenate([weight[k] for k in span], axis=1)
    rows = slice((e % 2) * SEQ, (e % 2 + 1) * SEQ)
    right = jnp.concatenate([grad[e // 2, k, rows, :] for k in span], axis=1)
    return lax.dot_general(left, right, LAST, preferred_element_type=jnp.float32)


def early_kernel(count, table, *refs):
    grads, pieces = refs[:2], refs[2:2 + count]
    out, queries, weight, grad, total, sems, out_sem = refs[2 + count:]
    groups = count // SIDE
    bounds = [SIDE * b for b in range(groups)] + [count]
    moving = [
        piece_copies(table, grads, pieces[bounds[b]:bounds[b + 1]], 2 * bounds[b], weight, grad, queries, sems.at[b])
        for b in range(groups)
    ]
    start(moving[0])
    start(moving[1])
    for b in range(groups):
        finish(moving[b])
        if b + 2 < groups:
            start(moving[b + 2])

        @pl.when(table[0] >= 0)
        def _():
            for e in range(4):
                value = product(weight, grad, range(2 * bounds[b], 2 * bounds[b + 1]), e)
                total[e] = value if b == 0 else value + total[e]
    write = pltpu.make_async_copy(total, out, out_sem)
    write.start()
    write.wait()


def late_kernel(count, table, *refs):
    grads, pieces = refs[:2], refs[2:2 + count]
    held, gate_own, gate_other, proj_out, in_own, in_other = refs[2 + count:8 + count]
    out_own, out_other, queries, weight, grad, total, value, gate, sem, total_sem = refs[8 + count:]
    moving = piece_copies(table, grads, pieces, 0, weight, grad, queries, sem)
    later = [pltpu.make_async_copy(held, total, total_sem)]
    later += [pltpu.make_async_copy(ref, gate.at[n], total_sem) for n, ref in enumerate((gate_own, gate_other))]
    start(moving)
    start(later)
    finish(moving)

    @pl.when(table[0] >= 0)
    def _():
        for e in range(4):
            value[e] = product(weight, grad, range(2 * count), e)

    finish(later)
    sides = []
    for e in range(4):
        v = gate[e // 2, :, (e % 2) * SEQ:(e % 2 + 1) * SEQ].astype(jnp.float32)
        up_grad = ((value[e] + total[e]) * (v / (1.0 + jnp.exp(-v)))).astype(jnp.bfloat16)
        sides.append(jnp.dot(proj_out[...], up_grad, preferred_element_type=jnp.float32))
    for e, out_side in enumerate(sides):
        in_side = (in_own, in_other)[e // 2][:, (e % 2) * SEQ:(e % 2 + 1) * SEQ]
        sketch = lax.dot_general(
            out_side, in_side, LAST, preferred_element_type=jnp.float32, precision=lax.Precision.HIGHEST
        )
        out = (out_own, out_other)[e // 2]
        out[(e % 2) * 32:(e % 2 + 1) * 32, :] = jnp.concatenate([sketch[:32], sketch[32:]], axis=1)


def grad_part(table, grads, pieces, tail=None):
    count = len(pieces)
    rows = grads[0].shape[0]
    smem, vmem, anywhere = [pl.BlockSpec(memory_space=m) for m in (pltpu.SMEM, pltpu.VMEM, pl.ANY)]
    total = ((4, HALF, SEQ), jnp.float32)
    queries = jax.ShapeDtypeStruct((2 * count, 64, LANES), jnp.bfloat16)
    scratch = [
        pltpu.VMEM((2 * count, HALF, LANES), jnp.bfloat16),
        pltpu.VMEM((2, 2 * count, rows, LANES), jnp.bfloat16),
        pltpu.VMEM(*total),
    ]
    if tail:
        kernel = late_kernel
        shapes, out_specs = [jax.ShapeDtypeStruct((64, LANES), jnp.float32)] * 2, [vmem] * 3
        in_specs = [anywhere] * (5 + count) + [vmem] * 3
        scratch += [pltpu.VMEM(*total), pltpu.VMEM((2, HALF, rows), jnp.bfloat16)]
        scratch += [pltpu.SemaphoreType.DMA, pltpu.SemaphoreType.DMA]
    else:
        kernel = early_kernel
        shapes, out_specs = [jax.ShapeDtypeStruct(*total)], [anywhere, vmem]
        in_specs = [anywhere] * (2 + count)
        scratch += [pltpu.SemaphoreType.DMA((count // SIDE,)), pltpu.SemaphoreType.DMA]
    return pl.pallas_call(
        lambda *refs: kernel(count, *refs),
        out_shape=shapes + [queries],
        in_specs=[smem] + in_specs,
        out_specs=out_specs,
        scratch_shapes=scratch,
        compiler_params=pltpu.CompilerParams(vmem_limit_bytes=VMEM_BYTES),
        cost_estimate=pl.CostEstimate(
            flops=8 * rows * HALF * count * LANES, bytes_accessed=count << 20, transcendentals=0
        ),
    )(table, *grads, *pieces, *(tail or ()))


def split3(value):
    high = value.astype(jnp.bfloat16)
    rest = value - high.astype(jnp.float32)
    mid = rest.astype(jnp.bfloat16)
    low = (rest - mid.astype(jnp.float32)).astype(jnp.bfloat16)
    return high, mid, low


def send_kernel(place, parts, payload, wide):
    sketch = parts[0]
    for k in range(1, 8):
        sketch = sketch + parts[k]
    wide[...] = sketch.astype(jnp.bfloat16).astype(jnp.float32)
    whole = wide[...]
    squares = jnp.sum(jnp.sum(whole * whole, axis=0, keepdims=True), axis=1, keepdims=True)
    parts = [v.astype(jnp.float32) for v in split3(jnp.broadcast_to(squares, (1, LANES)))]
    zero = jnp.zeros((1, LANES), jnp.float32)
    tails = [parts, [zero] * 3]
    first_col = place[0] * 4
    cols = [[wide[pl.ds(e * 32 + first_col + r, 1), :] for r in range(4)] for e in range(2)]
    for p in range(32):
        rows = []
        for e in range(2):
            rows += cols[e] + [wide[e * 32 + p:e * 32 + p + 1, :]] + tails[e]
        payload[p] = jnp.concatenate(rows, axis=0).astype(jnp.bfloat16)


def scores_kernel(count, place, order, wide, *refs):
    own_queries, other_queries = refs[:count], refs[count:2 * count]
    raw_scores, left = refs[2 * count:]
    left[...] = jnp.zeros_like(left)
    raw = []
    for q, queries in enumerate((own_queries, other_queries)):
        for k in range(32):
            for e in range(2):
                left[e:e + 1, k * LANES:(k + 1) * LANES] = wide[pl.ds(e * 32 + order[q * 32 + k], 1), :]
        right = jnp.concatenate([part[k] for part in queries for k in range(part.shape[0])], axis=1)
        raw.append(lax.dot_general(
            left[...].astype(jnp.bfloat16), right, LAST, preferred_element_type=jnp.float32
        ))
    even = (place[1] % 2) == 0
    raw_scores[...] = jnp.where(
        even, jnp.concatenate(raw, axis=1), jnp.concatenate(raw[::-1], axis=1)
    )


def send_part(place, sketches):
    smem, vmem = pl.BlockSpec(memory_space=pltpu.SMEM), pl.BlockSpec(memory_space=pltpu.VMEM)
    return pl.pallas_call(
        send_kernel,
        out_shape=(
            jax.ShapeDtypeStruct((32, 16, LANES), jnp.bfloat16),
            jax.ShapeDtypeStruct((64, LANES), jnp.float32),
        ),
        in_specs=[smem, vmem],
        out_specs=(vmem, vmem),
    )(place, sketches)


def scores_part(place, order, wide, own_queries, other_queries):
    smem, vmem = pl.BlockSpec(memory_space=pltpu.SMEM), pl.BlockSpec(memory_space=pltpu.VMEM)
    return pl.pallas_call(
        lambda *refs: scores_kernel(len(own_queries), *refs),
        out_shape=jax.ShapeDtypeStruct((8, LANES), jnp.float32),
        in_specs=[smem, smem] + [vmem] * (1 + 2 * len(own_queries)),
        out_specs=vmem,
        scratch_shapes=[pltpu.VMEM((8, 4096), jnp.float32)],
        cost_estimate=pl.CostEstimate(flops=2 * 8 * 4096 * 128, bytes_accessed=2 << 20, transcendentals=0),
    )(place, order, wide, *own_queries, *other_queries)


def gram_kernel(place, mine, raw_scores, gram, scores):
    t, dp = place[0], place[1]
    wide = mine[...].astype(jnp.float32)

    def stack(r):
        return jnp.concatenate([wide[:, r, :], wide[:, 8 + r, :]], axis=0).astype(jnp.bfloat16)

    trace = jnp.zeros((1, LANES), jnp.float32)
    for r in (7, 6, 5):
        trace = trace + jnp.sum(wide[:, r, :], axis=0, keepdims=True)
    row_part = stack(4)
    for r in range(4):
        raw = lax.dot_general(
            row_part, stack(r), (((0,), (0,)), ((), ())),
            preferred_element_type=jnp.float32,
        )
        rows = dp * LANES + lax.broadcasted_iota(jnp.int32, raw.shape, 0)
        cols = t * 512 + r * LANES + lax.broadcasted_iota(jnp.int32, raw.shape, 1)
        gram[:, r * LANES:(r + 1) * LANES] = raw * (4096.0 / trace) + jnp.where(rows == cols, 0.1, 0.0)
    scores[...] = raw_scores[:2, :] / jnp.sqrt(trace / 64.0)


def gram_part(place, mine, raw_scores):
    smem, vmem = pl.BlockSpec(memory_space=pltpu.SMEM), pl.BlockSpec(memory_space=pltpu.VMEM)
    return pl.pallas_call(
        gram_kernel,
        out_shape=(
            jax.ShapeDtypeStruct((LANES, 512), jnp.float32),
            jax.ShapeDtypeStruct((2, LANES), jnp.float32),
        ),
        in_specs=[smem, vmem, vmem],
        out_specs=(vmem, vmem),
    )(place, mine, raw_scores)


def halves(value, c, axis):
    size = value.shape[axis] // 2
    return [lax.dynamic_slice_in_dim(value, h * size, size, axis) for h in (c, 1 - c)]


def gather_pieces(down_weight, query, c):
    pair = (down_weight, query)
    first = jnp.stack([
        jnp.concatenate([halves(v, c, 0)[0] for v in values])
        for values in (pair, [core_swap(v) for v in pair])
    ])
    held = {(0, 0): first}
    held[0, 1], held[0, 2] = z_step(first, 1), z_step(first, -1)
    held[0, 3] = z_step(held[0, 1], 1)
    for n, (a, b) in enumerate(X_ORDER):
        source = held[1 if a == 3 else 0, b]
        if n >= IN_FLIGHT:
            source = after(source, held[X_ORDER[n - IN_FLIGHT]])
        held[a, b] = x_step(source, -1 if a == 2 else 1)
        if (a, b) == (3, 0):
            held[3, 2] = z_step(after(held[3, 0], held[0, 2]), -1)
    return held


def body(acts, output_grad, gate_act, down_weight, proj_in, proj_out, query):
    dp, tensor = lax.axis_index("dp"), lax.axis_index("tensor")
    x, z, c = dp // 8, (dp // 2) % SIDE, dp % 2
    hidden = down_weight.shape[0]

    held = gather_pieces(down_weight, query, c)
    grads = (output_grad, core_swap(after(output_grad, held[0, 0])))
    gate_keep, gate_give = halves(gate_act, c, 1)
    gates = (gate_keep.T, core_swap(after(gate_give, held[0, 0])).T)
    in_proj = lax.dot_general(proj_in, acts, LAST, preferred_element_type=jnp.float32)
    in_projs = (in_proj, core_swap(in_proj))
    proj_half = halves(proj_out, c, 1)[0].reshape(32, 2, hidden // 2)
    proj_half = jnp.concatenate([proj_half[:, k] for k in range(2)], axis=0)

    def columns(keys, core):
        sign = 1 - 2 * core
        return jnp.stack([
            dp_id(x + sign * FROM[a], z + sign * FROM[b], k) for a, b in keys for k in (core, 1 - core)
        ]).astype(jnp.int32)

    early, late = ARRIVAL[:13], ARRIVAL[13:]
    total, early_queries = grad_part(columns(early, c), grads, [held[key] for key in early])
    own_part, other_part, late_queries = grad_part(
        columns(late, c), grads, [held[key] for key in late], (total, *gates, proj_half, *in_projs)
    )
    own_queries = [early_queries, late_queries]
    other_queries = [core_swap(part) for part in own_queries]
    order = jnp.concatenate([columns(ARRIVAL, c), columns(ARRIVAL, 1 - c)])
    eight = lax.optimization_barrier(jnp.broadcast_to(own_part[None], (8,) + own_part.shape))
    sketches = lax.all_to_all(eight + core_swap(other_part)[None], "tensor", 0, 0)
    place = jnp.stack([tensor, dp]).astype(jnp.int32)
    payload, wide = send_part(place, sketches)
    mine = lax.all_to_all(payload, "dp", 0, 0)
    raw_scores = scores_part(place, order, wide, own_queries, other_queries)
    return gram_part(place, mine, raw_scores)


def solution(mesh):
    placed = (
        P("dp", None),
        P("dp", None),
        P("dp", "tensor"),
        P("tensor", "dp"),
        P(),
        P(None, "tensor"),
        P("tensor", "dp"),
    )
    return jax.shard_map(
        body,
        mesh=mesh,
        in_specs=placed,
        out_specs=(P("dp", "tensor"), P("dp", "tensor")),
        check_vma=False,
    )
```

```python
import jax
import jax.numpy as jnp
from jax import lax
from jax.experimental import pallas as pl
from jax.experimental.pallas import tpu as pltpu
from jax.sharding import PartitionSpec as P

SEQ = 256
SIDE = 4
LANES = 128
HALF = 896
VMEM_BYTES = 36 << 20
LAST = (((1,), (1,)), ((), ()))


def dp_id(x, z, c):
    return ((x % SIDE) * SIDE + z % SIDE) * 2 + c


PLACES = [(x, z, c) for x in range(SIDE) for z in range(SIDE) for c in range(2)]


FROM = (0, -1, 1, -2)
X_ORDER = [
    (1, 0), (2, 0), (3, 0), (1, 1), (2, 1), (1, 2), (2, 2), (3, 1), (1, 3), (2, 3), (3, 3),
]
IN_FLIGHT = 3
ARRIVAL = [(0, 0), (0, 1), (0, 2), (1, 0), (2, 0), (3, 0), (1, 1), (2, 1), (1, 2), (2, 2), (3, 1), (0, 3)]
ARRIVAL += [(1, 3), (3, 2), (2, 3), (3, 3)]


def dp_move(value, where):
    return lax.ppermute(value, "dp", [(dp_id(*s), dp_id(*where(*s))) for s in PLACES])


def x_step(value, way):
    return dp_move(value, lambda x, z, c: (x + way * (1 - 2 * c), z, c))


def z_step(value, way):
    return dp_move(value, lambda x, z, c: (x, z + way * (1 - 2 * c), c))


def core_swap(value):
    return dp_move(value, lambda x, z, c: (x, z, 1 - c))


def tensor_swap(value, bit):
    return lax.ppermute(value, "tensor", [(t, t ^ bit) for t in range(8)])


def after(value, *others):
    return lax.optimization_barrier((value,) + others)[0]


def piece_copies(table, grads, pieces, first, weight, grad, queries, sem):
    made = []
    for p, piece in enumerate(pieces):
        k = first + 2 * p
        made.append((piece.at[:, :HALF], weight.at[k:k + 2]))
        made.append((piece.at[:, HALF:], queries.at[k:k + 2]))
    for k in range(first, first + 2 * len(pieces)):
        span = pl.ds(pl.multiple_of(table[k] * LANES, LANES), LANES)
        made += [(grads[side].at[:, span], grad.at[side, k]) for side in range(2)]
    return [pltpu.make_async_copy(x, y, sem) for x, y in made]


def start(copies):
    for copy in copies:
        copy.start()


def finish(copies):
    for copy in copies:
        copy.wait()


def product(weight, grad, span, e):
    left = jnp.concatenate([weight[k] for k in span], axis=1)
    rows = slice((e % 2) * SEQ, (e % 2 + 1) * SEQ)
    right = jnp.concatenate([grad[e // 2, k, rows, :] for k in span], axis=1)
    return lax.dot_general(left, right, LAST, preferred_element_type=jnp.float32)


def early_kernel(count, table, *refs):
    grads, pieces = refs[:2], refs[2:2 + count]
    out, queries, weight, grad, total, sems, out_sem = refs[2 + count:]
    groups = count // SIDE
    bounds = [SIDE * b for b in range(groups)] + [count]
    moving = [
        piece_copies(table, grads, pieces[bounds[b]:bounds[b + 1]], 2 * bounds[b], weight, grad, queries, sems.at[b])
        for b in range(groups)
    ]
    start(moving[0])
    start(moving[1])
    for b in range(groups):
        finish(moving[b])
        if b + 2 < groups:
            start(moving[b + 2])

        @pl.when(table[0] >= 0)
        def _():
            for e in range(4):
                value = product(weight, grad, range(2 * bounds[b], 2 * bounds[b + 1]), e)
                total[e] = value if b == 0 else value + total[e]
    write = pltpu.make_async_copy(total, out, out_sem)
    write.start()
    write.wait()


def late_kernel(count, table, *refs):
    grads, pieces = refs[:2], refs[2:2 + count]
    held, gate_own, gate_other, proj_out, in_own, in_other = refs[2 + count:8 + count]
    out_own, out_other, queries, weight, grad, total, value, gate, sem, total_sem = refs[8 + count:]
    moving = piece_copies(table, grads, pieces, 0, weight, grad, queries, sem)
    later = [pltpu.make_async_copy(held, total, total_sem)]
    later += [pltpu.make_async_copy(ref, gate.at[n], total_sem) for n, ref in enumerate((gate_own, gate_other))]
    start(moving)
    start(later)
    finish(moving)

    @pl.when(table[0] >= 0)
    def _():
        for e in range(4):
            value[e] = product(weight, grad, range(2 * count), e)

    finish(later)
    sides = []
    for e in range(4):
        v = gate[e // 2, :, (e % 2) * SEQ:(e % 2 + 1) * SEQ].astype(jnp.float32)
        up_grad = ((value[e] + total[e]) * (v / (1.0 + jnp.exp(-v)))).astype(jnp.bfloat16)
        sides.append(jnp.dot(proj_out[...], up_grad, preferred_element_type=jnp.float32))
    for e, out_side in enumerate(sides):
        in_side = (in_own, in_other)[e // 2][:, (e % 2) * SEQ:(e % 2 + 1) * SEQ]
        sketch = lax.dot_general(
            out_side, in_side, LAST, preferred_element_type=jnp.float32, precision=lax.Precision.HIGHEST
        )
        rows, block = slice((e % 2) * 32, (e % 2 + 1) * 32), jnp.concatenate([sketch[:32], sketch[32:]], axis=1)
        if e < 2:
            for peer in range(8):
                out_own[peer, rows, :] = block
        else:
            out_other[rows, :] = block


def grad_part(table, grads, pieces, tail=None):
    count = len(pieces)
    rows = grads[0].shape[0]
    smem, vmem, anywhere = [pl.BlockSpec(memory_space=m) for m in (pltpu.SMEM, pltpu.VMEM, pl.ANY)]
    total = ((4, HALF, SEQ), jnp.float32)
    queries = jax.ShapeDtypeStruct((2 * count, 64, LANES), jnp.bfloat16)
    scratch = [
        pltpu.VMEM((2 * count, HALF, LANES), jnp.bfloat16),
        pltpu.VMEM((2, 2 * count, rows, LANES), jnp.bfloat16),
        pltpu.VMEM(*total),
    ]
    if tail:
        kernel = late_kernel
        shapes, out_specs = [jax.ShapeDtypeStruct(s, jnp.float32) for s in ((8, 64, LANES), (64, LANES))], [vmem] * 3
        in_specs = [anywhere] * (5 + count) + [vmem] * 3
        scratch += [pltpu.VMEM(*total), pltpu.VMEM((2, HALF, rows), jnp.bfloat16)]
        scratch += [pltpu.SemaphoreType.DMA, pltpu.SemaphoreType.DMA]
    else:
        kernel = early_kernel
        shapes, out_specs = [jax.ShapeDtypeStruct(*total)], [anywhere, vmem]
        in_specs = [anywhere] * (2 + count)
        scratch += [pltpu.SemaphoreType.DMA((count // SIDE,)), pltpu.SemaphoreType.DMA]
    return pl.pallas_call(
        lambda *refs: kernel(count, *refs),
        out_shape=shapes + [queries],
        in_specs=[smem] + in_specs,
        out_specs=out_specs,
        scratch_shapes=scratch,
        compiler_params=pltpu.CompilerParams(vmem_limit_bytes=VMEM_BYTES),
        cost_estimate=pl.CostEstimate(
            flops=8 * rows * HALF * count * LANES, bytes_accessed=count << 20, transcendentals=0
        ),
    )(table, *grads, *pieces, *(tail or ()))


def split3(value):
    high = value.astype(jnp.bfloat16)
    rest = value - high.astype(jnp.float32)
    mid = rest.astype(jnp.bfloat16)
    low = (rest - mid.astype(jnp.float32)).astype(jnp.bfloat16)
    return high, mid, low


def send_kernel(place, parts, payload, wide):
    sketch = parts[0]
    for k in range(1, 8):
        sketch = sketch + parts[k]
    wide[...] = sketch.astype(jnp.bfloat16).astype(jnp.float32)
    whole = wide[...]
    squares = jnp.sum(jnp.sum(whole * whole, axis=0, keepdims=True), axis=1, keepdims=True)
    parts = [v.astype(jnp.float32) for v in split3(jnp.broadcast_to(squares, (1, LANES)))]
    zero = jnp.zeros((1, LANES), jnp.float32)
    tails = [parts, [zero] * 3]
    first_col = place[0] * 4
    cols = [[wide[pl.ds(e * 32 + first_col + r, 1), :] for r in range(4)] for e in range(2)]
    for p in range(32):
        rows = []
        for e in range(2):
            rows += cols[e] + [wide[e * 32 + p:e * 32 + p + 1, :]] + tails[e]
        payload[p] = jnp.concatenate(rows, axis=0).astype(jnp.bfloat16)


def scores_kernel(count, place, order, wide, *refs):
    own_queries, other_queries = refs[:count], refs[count:2 * count]
    raw_scores, left = refs[2 * count:]
    left[...] = jnp.zeros_like(left)
    raw = []
    for q, queries in enumerate((own_queries, other_queries)):
        for k in range(32):
            for e in range(2):
                left[e:e + 1, k * LANES:(k + 1) * LANES] = wide[pl.ds(e * 32 + order[q * 32 + k], 1), :]
        right = jnp.concatenate([part[k] for part in queries for k in range(part.shape[0])], axis=1)
        raw.append(lax.dot_general(
            left[...].astype(jnp.bfloat16), right, LAST, preferred_element_type=jnp.float32
        ))
    even = (place[1] % 2) == 0
    raw_scores[...] = jnp.where(
        even, jnp.concatenate(raw, axis=1), jnp.concatenate(raw[::-1], axis=1)
    )


def send_part(place, sketches):
    smem, vmem = pl.BlockSpec(memory_space=pltpu.SMEM), pl.BlockSpec(memory_space=pltpu.VMEM)
    return pl.pallas_call(
        send_kernel,
        out_shape=(
            jax.ShapeDtypeStruct((32, 16, LANES), jnp.bfloat16),
            jax.ShapeDtypeStruct((64, LANES), jnp.float32),
        ),
        in_specs=[smem, vmem],
        out_specs=(vmem, vmem),
    )(place, sketches)


def scores_part(place, order, wide, own_queries, other_queries):
    smem, vmem = pl.BlockSpec(memory_space=pltpu.SMEM), pl.BlockSpec(memory_space=pltpu.VMEM)
    return pl.pallas_call(
        lambda *refs: scores_kernel(len(own_queries), *refs),
        out_shape=jax.ShapeDtypeStruct((8, LANES), jnp.float32),
        in_specs=[smem, smem] + [vmem] * (1 + 2 * len(own_queries)),
        out_specs=vmem,
        scratch_shapes=[pltpu.VMEM((8, 4096), jnp.float32)],
        cost_estimate=pl.CostEstimate(flops=2 * 8 * 4096 * 128, bytes_accessed=2 << 20, transcendentals=0),
    )(place, order, wide, *own_queries, *other_queries)


def gram_kernel(place, mine, raw_scores, gram, scores):
    t, dp = place[0], place[1]
    wide = mine[...].astype(jnp.float32)

    def stack(r):
        return jnp.concatenate([wide[:, r, :], wide[:, 8 + r, :]], axis=0).astype(jnp.bfloat16)

    trace = jnp.zeros((1, LANES), jnp.float32)
    for r in (7, 6, 5):
        trace = trace + jnp.sum(wide[:, r, :], axis=0, keepdims=True)
    row_part = stack(4)
    for r in range(4):
        raw = lax.dot_general(
            row_part, stack(r), (((0,), (0,)), ((), ())),
            preferred_element_type=jnp.float32,
        )
        rows = dp * LANES + lax.broadcasted_iota(jnp.int32, raw.shape, 0)
        cols = t * 512 + r * LANES + lax.broadcasted_iota(jnp.int32, raw.shape, 1)
        gram[:, r * LANES:(r + 1) * LANES] = raw * (4096.0 / trace) + jnp.where(rows == cols, 0.1, 0.0)
    scores[...] = raw_scores[:2, :] / jnp.sqrt(trace / 64.0)


def gram_part(place, mine, raw_scores):
    smem, vmem = pl.BlockSpec(memory_space=pltpu.SMEM), pl.BlockSpec(memory_space=pltpu.VMEM)
    return pl.pallas_call(
        gram_kernel,
        out_shape=(
            jax.ShapeDtypeStruct((LANES, 512), jnp.float32),
            jax.ShapeDtypeStruct((2, LANES), jnp.float32),
        ),
        in_specs=[smem, vmem, vmem],
        out_specs=(vmem, vmem),
    )(place, mine, raw_scores)


def halves(value, c, axis):
    size = value.shape[axis] // 2
    return [lax.dynamic_slice_in_dim(value, h * size, size, axis) for h in (c, 1 - c)]


def gather_pieces(down_weight, query, c):
    pair = (down_weight, query)
    first = jnp.stack([
        jnp.concatenate([halves(v, c, 0)[0] for v in values])
        for values in (pair, [core_swap(v) for v in pair])
    ])
    held = {(0, 0): first}
    held[0, 1], held[0, 2] = z_step(first, 1), z_step(first, -1)
    held[0, 3] = z_step(held[0, 1], 1)
    for n, (a, b) in enumerate(X_ORDER):
        source = held[1 if a == 3 else 0, b]
        if n >= IN_FLIGHT:
            source = after(source, held[X_ORDER[n - IN_FLIGHT]])
        held[a, b] = x_step(source, -1 if a == 2 else 1)
        if (a, b) == (3, 0):
            held[3, 2] = z_step(after(held[3, 0], held[0, 2]), -1)
    return held


def body(acts, output_grad, gate_act, down_weight, proj_in, proj_out, query):
    dp, tensor = lax.axis_index("dp"), lax.axis_index("tensor")
    x, z, c = dp // 8, (dp // 2) % SIDE, dp % 2
    hidden = down_weight.shape[0]

    held = gather_pieces(down_weight, query, c)
    grads = (output_grad, core_swap(after(output_grad, held[0, 0])))
    gate_keep, gate_give = halves(gate_act, c, 1)
    gates = (gate_keep.T, core_swap(after(gate_give, held[0, 0])).T)
    in_proj = lax.dot_general(proj_in, acts, LAST, preferred_element_type=jnp.float32)
    in_projs = (in_proj, core_swap(in_proj))
    proj_half = halves(proj_out, c, 1)[0].reshape(32, 2, hidden // 2)
    proj_half = jnp.concatenate([proj_half[:, k] for k in range(2)], axis=0)

    def columns(keys, core):
        sign = 1 - 2 * core
        return jnp.stack([
            dp_id(x + sign * FROM[a], z + sign * FROM[b], k) for a, b in keys for k in (core, 1 - core)
        ]).astype(jnp.int32)

    early, late = ARRIVAL[:13], ARRIVAL[13:]
    total, early_queries = grad_part(columns(early, c), grads, [held[key] for key in early])
    own_part, other_part, late_queries = grad_part(
        columns(late, c), grads, [held[key] for key in late], (total, *gates, proj_half, *in_projs)
    )
    own_queries = [early_queries, late_queries]
    other_queries = [core_swap(part) for part in own_queries]
    order = jnp.concatenate([columns(ARRIVAL, c), columns(ARRIVAL, 1 - c)])
    sketches = lax.all_to_all(own_part + core_swap(other_part)[None], "tensor", 0, 0)
    place = jnp.stack([tensor, dp]).astype(jnp.int32)
    payload, wide = send_part(place, sketches)
    mine = lax.all_to_all(payload, "dp", 0, 0)
    raw_scores = scores_part(place, order, wide, own_queries, other_queries)
    return gram_part(place, mine, raw_scores)


def solution(mesh):
    placed = (
        P("dp", None),
        P("dp", None),
        P("dp", "tensor"),
        P("tensor", "dp"),
        P(),
        P(None, "tensor"),
        P("tensor", "dp"),
    )
    return jax.shard_map(
        body,
        mesh=mesh,
        in_specs=placed,
        out_specs=(P("dp", "tensor"), P("dp", "tensor")),
        check_vma=False,
    )
```
